32 devices in a mesh: band: 8 (over z, y), member: 4 (over x, core).
Axes of the slice: x: 2, y: 2, z: 4, core: 2. Of those that a mesh axis runs over, the one named last changes fastest.
Arguments:
- targets: float32 [32, 64, 4096], P(('band', 'member')), may hold values from -6 to 6
- sources: float32 [16, 64, 4096], P('band', 'member'), may hold values from -6 to 6
Outputs:
- exchange: float32 [32, 64, 4096], P(('band', 'member'))
The draws below stay inside these ranges and needn't reach their ends.
All inputs are finite; a program needn't handle non-finite values.
Results may differ from the reference program's by a relative error of at most 0.0003.
Values sent between devices are 32-bit elements; how exact they have to be, the bound alone decides.
No kernel may reach another device: no remote copies, remote signals or barrier semaphores. Data moves between devices by JAX's collectives and lax.ppermute only.
A program may use at most 64 MiB of HBM per device.

```python
import jax
import jax.numpy as jnp
from jax import lax

G = 64
TGT_DEV = 1
SRC_BLOCK = 2
STOPS = 2
TARGETS = 32
SOURCES = 16
N_BAND = 8
N_MEMBER = 4


def level_of(key, extent, shards, least, largest):
    level = 1.0
    for position, parts in shards:
        heights = jax.random.uniform(jax.random.fold_in(jax.random.fold_in(key, 6), position), (parts,), jnp.float32, least / len(shards), largest / len(shards))
        level = level * jnp.repeat(jnp.exp(heights), extent[position] // parts).reshape((-1,) + (1,) * (len(extent) - 1 - position))
    return level


def centred(own_key, extent, scale, limit, shards=(), kind=jnp.bfloat16):
    loudness = level_of(own_key, extent, shards, -0.22, 0.18) if shards else 1.0
    values = jax.random.normal(own_key, extent, jnp.float32) * scale * loudness
    return jnp.minimum(jnp.maximum(values, -limit), limit).astype(kind)


def setup_inputs(seed: int = 0) -> dict:
    key_of = jax.random.split(jax.random.key(seed), 3)
    return {
        "targets": centred(key_of[0], (TARGETS, G, G * G), 1.0, 6.0, ((0, 32),), jnp.float32),
        "sources": centred(key_of[1], (SOURCES, G, G * G), 1.0, 6.0, ((0, 8), (1, 4)), jnp.float32),
    }


def sine_axis(field, axis):
    moved = jnp.moveaxis(field, axis, -1)
    count = moved.shape[-1]
    edge = jnp.zeros(moved.shape[:-1] + (1,), moved.dtype)
    extended = jnp.concatenate([edge, moved, edge, -moved[..., ::-1]], axis=-1)
    spectrum = jnp.fft.rfft(extended, axis=-1)
    result = (-0.5 * jnp.imag(spectrum[..., 1:count + 1])).astype(moved.dtype)
    return jnp.moveaxis(result, -1, axis)


def sine_three(field):
    for axis in range(3):
        field = sine_axis(field, axis)
    return field


def inverse_table(dtype):
    wave = jnp.arange(G, dtype=dtype) + 1.0
    single = 4.0 * jnp.sin(jnp.pi * wave / (2.0 * (G + 1))) ** 2
    eigen = single[:, None, None] + single[None, :, None] + single[None, None, :]
    return (2.0 / (G + 1)) ** 3 / eigen


def reference(targets, sources):
    group = N_MEMBER * TGT_DEV
    inverse_eigen = inverse_table(targets.dtype)
    bands = (jnp.arange(TARGETS) // group).astype(jnp.int32)

    def one_target(item):
        target, band = item
        cube = target.reshape(G, G, G)
        total = jnp.zeros((G, G, G), targets.dtype)
        for stop in range(STOPS):
            block = ((band - stop) % N_BAND).astype(jnp.int32)
            chosen = lax.dynamic_slice_in_dim(sources, (block * SRC_BLOCK).astype(jnp.int32), SRC_BLOCK, 0)
            for member in range(SRC_BLOCK):
                source = chosen[member].reshape(G, G, G)
                potential = sine_three(sine_three(cube * source) * inverse_eigen)
                total = total - source * potential
        return total.reshape(G, G * G)

    return lax.map(one_target, (targets, bands))
```

```python
import functools

import jax
import jax.numpy as jnp
import numpy as np
from jax import lax
from jax.experimental import pallas as pl
from jax.experimental.pallas import tpu as pltpu
from jax.sharding import PartitionSpec as P

STOPS = 2
LANES = 128

dot = functools.partial(jnp.dot, preferred_element_type=jnp.float32)


def cat(values, axis):
    return jnp.concatenate(values, axis=axis)


def split(values):
    high = values.astype(jnp.bfloat16)
    low = (values - high.astype(jnp.float32)).astype(jnp.bfloat16)
    return high, low


def tables(cells):
    wave = np.arange(cells) + 1.0
    sine = np.sin(np.pi * wave[:, None] * wave[None, :] / (cells + 1)).astype(np.float32)
    high = sine.astype(jnp.bfloat16)
    low = (sine - high.astype(np.float32)).astype(jnp.bfloat16)
    none = np.zeros_like(high)
    pair_high = np.block([[high, none], [none, high]])
    pair_low = np.block([[low, none], [none, low]])
    lane_table = np.block([[pair_high, pair_low], [pair_high, pair_low]])
    order = np.concatenate([np.arange(0, cells, 2), np.arange(1, cells, 2)])
    row_table = np.concatenate([high, high, low], 1)
    column_table = np.concatenate([high[:, order], high[:, order], low[:, order]], 1)
    back_table = np.concatenate([high[order], high[order], low[order]], 1)
    single = 4.0 * np.sin(np.pi * wave / (2.0 * (cells + 1))) ** 2
    eigen = single[:, None, None] + single[None, :, None] + single[None, None, :]
    inverse = (2.0 / (cells + 1)) ** 3 / eigen
    inverse = inverse.reshape(cells // 2, 2, cells, cells).transpose(0, 2, 1, 3)
    inverse = inverse.reshape(cells * cells // 2, 2 * cells).astype(np.float32)
    return lane_table, row_table, column_table, back_table, inverse


def solve_kernel(cells, parts, first, *refs):
    count = len(parts)
    pieces, refs = refs[:count], refs[count:]
    target, refs = refs[0], refs[1:]
    if not first:
        before, refs = refs[0], refs[1:]
    lane_table, row_table, column_table, back_table, inverse, out, source, planes, columns, sems = refs
    pairs = cells // 2
    plane_pitch, column_pitch = cells + 8, pairs + 8
    me = lax.axis_index("member")

    copies = []
    for number, (index, distance) in enumerate(parts):
        rows = pieces[number].shape[1]
        start = 0 if distance is None else pl.multiple_of((me ^ distance) * rows, 8)
        copy = pltpu.make_async_copy(pieces[number].at[index], source.at[pl.ds(start, rows), :], sems.at[number])
        copy.start()
        copies.append(copy)
    for copy in copies:
        copy.wait()

    low = lax.broadcasted_iota(jnp.int32, (pairs, LANES), 1) < cells

    def along_lanes(values):
        high, rest = split(values)
        product = dot(cat([high, rest], 1), lane_table[...])
        return product[:, :LANES] + product[:, LANES:]

    def along_rows(table, values):
        high, rest = split(values)
        return dot(table[...], cat([high, rest, high], 0))

    def tile(u):
        return slice(u * LANES, (u + 1) * LANES)

    def block(u):
        return slice(u * cells, (u + 1) * cells)

    field = along_lanes(cat([target[:, tile(u)] * source[:, tile(u)] for u in range(pairs)], 0))
    field = along_rows(row_table, cat([field[block(u)] for u in range(pairs)], 1))
    for u in range(pairs):
        planes[pl.ds(u * plane_pitch, cells), :] = field[:, tile(u)]

    turned = []
    for u in range(pairs):
        even = planes[pl.ds(2 * u, pairs, plane_pitch), :]
        odd = planes[pl.ds(2 * u + 1, pairs, plane_pitch), :]
        upper = jnp.where(low, even, pltpu.roll(odd, cells, 1))
        lower = jnp.where(low, pltpu.roll(even, cells, 1), odd)
        turned.append(cat([upper, lower], 0))
    field = along_rows(column_table, cat(turned, 1))
    field = field * cat([inverse[block(u), :] for u in range(pairs)], 1)
    field = along_rows(back_table, field)
    for u in range(pairs):
        upper, lower = field[:pairs, tile(u)], field[pairs:, tile(u)]
        columns[pl.ds(2 * u * column_pitch, pairs), :] = jnp.where(low, upper, pltpu.roll(lower, cells, 1))
        columns[pl.ds((2 * u + 1) * column_pitch, pairs), :] = jnp.where(low, pltpu.roll(upper, cells, 1), lower)

    field = along_rows(row_table, cat([columns[pl.ds(u, cells, column_pitch), :] for u in range(pairs)], 1))
    field = along_lanes(cat([field[:, tile(u)] for u in range(pairs)], 0))
    for u in range(pairs):
        term = source[:, tile(u)] * field[block(u)]
        out[:, tile(u)] = -term if first else before[:, tile(u)] - term


def solve(target, parts, total, constants):
    cells, plane = target.shape
    vmem = pl.BlockSpec(memory_space=pltpu.VMEM)
    anywhere = pl.BlockSpec(memory_space=pl.ANY)
    arrays = [part[0] for part in parts]
    layout = tuple(part[1:] for part in parts)
    operands = [target] + ([] if total is None else [total]) + list(constants)
    return pl.pallas_call(
        functools.partial(solve_kernel, cells, layout, total is None),
        out_shape=jax.ShapeDtypeStruct((cells, plane), jnp.float32),
        in_specs=[anywhere] * len(arrays) + [vmem] * len(operands),
        out_specs=vmem,
        scratch_shapes=[
            pltpu.VMEM((cells, plane), jnp.float32),
            pltpu.VMEM((cells // 2 * (cells + 8), LANES), jnp.float32),
            pltpu.VMEM((cells * (cells // 2 + 8), LANES), jnp.float32),
            pltpu.SemaphoreType.DMA((len(arrays),)),
        ],
        compiler_params=pltpu.CompilerParams(vmem_limit_bytes=24 << 20),
    )(*arrays, *operands)


def from_member(piece, distance):
    return lax.ppermute(piece, "member", [(i ^ distance, i) for i in range(lax.axis_size("member"))])


def from_band(piece):
    count = lax.axis_size("band")
    return lax.ppermute(piece, "band", [((i - 1) % count, i) for i in range(count)])


def body(targets, sources):
    cells = targets.shape[1]
    count = sources.shape[0]
    target = targets[0]
    constants = [jnp.asarray(table) for table in tables(cells)]
    total = None
    if lax.axis_size("member") != 4:
        slab = sources
        for stop in range(STOPS):
            if stop > 0:
                slab = from_band(slab)
            whole = lax.all_gather(slab, "member", axis=1, tiled=True)
            for index in range(count):
                total = solve(target, [(whole, index, None)], total, constants)
        return total[None]
    near = from_member(sources, 1)
    across = from_member(sources, 2)
    far = from_band(sources)
    far_across = from_member(far, 2)
    across_near = from_member(across, 1)
    far_near = from_member(far, 1)
    far_across_near = from_member(far_across, 1)
    for group in ((sources, near, across, across_near), (far, far_near, far_across, far_across_near)):
        for index in range(count):
            parts = [(piece, index, distance) for distance, piece in enumerate(group)]
            total = solve(target, parts, total, constants)
    return total[None]


def solution(mesh):
    placed = (P(("band", "member"), None, None), P("band", "member", None))
    return jax.shard_map(
        body,
        mesh=mesh,
        in_specs=placed,
        out_specs=P(("band", "member"), None, None),
        check_vma=False,
    )
```

```python
import functools

import jax
import jax.numpy as jnp
import numpy as np
from jax import lax
from jax.experimental import pallas as pl
from jax.experimental.pallas import tpu as pltpu
from jax.sharding import PartitionSpec as P

STOPS = 2
LANES = 128
ROWS = 8
CHUNKS = 2

dot = functools.partial(jnp.dot, preferred_element_type=jnp.float32)


def cat(values, axis):
    return jnp.concatenate(values, axis=axis)


def split(values):
    high = values.astype(jnp.bfloat16)
    low = (values - high.astype(jnp.float32)).astype(jnp.bfloat16)
    return high, low


def tables(cells, layouts):
    wave = np.arange(cells) + 1.0
    sine = np.sin(np.pi * wave[:, None] * wave[None, :] / (cells + 1)).astype(np.float32)
    high = sine.astype(jnp.bfloat16)
    low = (sine - high.astype(np.float32)).astype(jnp.bfloat16)
    none = np.zeros_like(high)
    pair_high = np.block([[high, none], [none, high]])
    pair_low = np.block([[low, none], [none, low]])
    lane_table = np.block([[pair_high, pair_low], [pair_high, pair_low]])
    order = np.concatenate([np.arange(0, cells, 2), np.arange(1, cells, 2)])
    plane_table = np.stack([np.concatenate([high[:, rows], high[:, rows], low[:, rows]], 1) for rows in layouts])
    plane_back_table = np.stack([np.concatenate([high[rows], high[rows], low[rows]], 1) for rows in layouts])
    column_table = np.concatenate([high[:, order], high[:, order], low[:, order]], 1)
    back_table = np.concatenate([high[order], high[order], low[order]], 1)
    single = 4.0 * np.sin(np.pi * wave / (2.0 * (cells + 1))) ** 2
    eigen = single[:, None, None] + single[None, :, None] + single[None, None, :]
    inverse = (2.0 / (cells + 1)) ** 3 / eigen
    inverse = inverse.reshape(cells // 2, 2, cells, cells).transpose(0, 2, 1, 3)
    inverse = inverse.reshape(cells * cells // 2, 2 * cells).astype(np.float32)
    return lane_table, plane_table, plane_back_table, column_table, back_table, inverse


def prepare_kernel(count, *refs):
    outs, sems = refs[-count - 1:-1], refs[-1]
    copies = [pltpu.make_async_copy(refs[i], outs[i], sems.at[i]) for i in range(count)]
    for copy in copies:
        copy.start()
    for copy in copies:
        copy.wait()


def in_vmem(arrays, *earlier):
    return pl.pallas_call(
        functools.partial(prepare_kernel, len(arrays)),
        out_shape=[pltpu.VMEM(array.shape, array.dtype) for array in arrays],
        in_specs=[pl.BlockSpec(memory_space=pltpu.HBM)] * len(arrays) + [pl.BlockSpec(memory_space=pl.ANY)] * len(earlier),
        out_specs=[pl.BlockSpec(memory_space=pltpu.VMEM)] * len(arrays),
        scratch_shapes=[pltpu.SemaphoreType.DMA((len(arrays),))],
        compiler_params=pltpu.CompilerParams(vmem_limit_bytes=1 << 20),
    )(*[pltpu.with_memory_space_constraint(array, pltpu.HBM) for array in arrays], *earlier)


def parts_kernel(source, *refs):
    outs, sems = refs[:-1], refs[-1]
    copies = [pltpu.make_async_copy(source.at[pl.ds(i, 1)], out, sems.at[i]) for i, out in enumerate(outs)]
    for copy in copies:
        copy.start()
    for copy in copies:
        copy.wait()


def in_vmem_parts(sources):
    count, extent, plane = sources.shape
    return pl.pallas_call(
        parts_kernel,
        out_shape=[pltpu.VMEM((1, extent, plane), sources.dtype)] * count,
        in_specs=[pl.BlockSpec(memory_space=pltpu.HBM)],
        out_specs=[pl.BlockSpec(memory_space=pltpu.VMEM)] * count,
        scratch_shapes=[pltpu.SemaphoreType.DMA((count,))],
        compiler_params=pltpu.CompilerParams(vmem_limit_bytes=1 << 20),
    )(pltpu.with_memory_space_constraint(sources, pltpu.HBM))


def parts_kernel(source, *refs):
    outs, sems = refs[:-1], refs[-1]
    copies = [pltpu.make_async_copy(source.at[pl.ds(i, 1)], out, sems.at[i]) for i, out in enumerate(outs)]
    for copy in copies:
        copy.start()
    for copy in copies:
        copy.wait()


def in_vmem_parts(sources):
    count, extent, plane = sources.shape
    return pl.pallas_call(
        parts_kernel,
        out_shape=[pltpu.VMEM((1, extent, plane), sources.dtype)] * count,
        in_specs=[pl.BlockSpec(memory_space=pltpu.HBM)],
        out_specs=[pl.BlockSpec(memory_space=pltpu.VMEM)] * count,
        scratch_shapes=[pltpu.SemaphoreType.DMA((count,))],
        compiler_params=pltpu.CompilerParams(vmem_limit_bytes=1 << 20),
    )(pltpu.with_memory_space_constraint(sources, pltpu.HBM))


def solve_kernel(cells, groups, spare, first, last, *refs):
    sources = len(groups)
    pieces = []
    for group in groups:
        pieces.append(refs[:len(group)])
        refs = refs[len(group):]
    refs = refs[spare:]
    target, refs = refs[0], refs[1:]
    if not first:
        before, refs = refs[0], refs[1:]
    lane_table, plane_table, plane_back_table, column_table, back_table, inverse, out, planes, columns = refs[:9]
    pairs = cells // 2
    plane_pitch, column_pitch = cells + 8, pairs + 8
    me = lax.axis_index("member")
    extent = cells // lax.axis_size("member")
    places = [
        [(number, index, row) for number, (index, _, _, count) in enumerate(group) for row in range(0, count, ROWS)]
        for group in groups
    ]
    layout = [
        (distance, offset + row) for _, distance, offset, count in groups[0] for row in range(0, count, ROWS)
    ]

    def rows(segment):
        distance, offset = layout[segment]
        start = offset if distance is None else (me ^ distance) * extent + offset
        return pl.ds(pl.multiple_of(start, ROWS), ROWS)

    order = 0 if layout[0][0] is None else me
    low = lax.broadcasted_iota(jnp.int32, (pairs, LANES), 1) < cells
    every = [(j, u) for j in range(sources) for u in range(pairs)]

    def along_lanes(values):
        high, rest = split(values)
        product = dot(cat([high, rest], 1), lane_table[...])
        return product[:, :LANES] + product[:, LANES:]

    def along_rows(table, values):
        high, rest = split(values)
        return dot(table, cat([high, rest, high], 0))

    def tile(u):
        return slice(u * LANES, (u + 1) * LANES)

    def block(u):
        return slice(u * cells, (u + 1) * cells)

    def piece(j, segment, u):
        number, index, row = places[j][segment]
        return pieces[j][number][index, row:row + ROWS, tile(u)]

    segments = range(len(layout))
    field = [target[rows(segment), tile(u)] * piece(j, segment, u) for j, u in every for segment in segments]
    field = along_lanes(cat(field, 0))
    field = along_rows(plane_table[order], cat([field[block(i)] for i in range(len(every))], 1))
    for i, (j, u) in enumerate(every):
        planes[j, pl.ds(u * plane_pitch, cells), :] = field[:, tile(i)]

    turned = []
    for j, u in every:
        even = planes[j, pl.ds(2 * u, pairs, plane_pitch), :]
        odd = planes[j, pl.ds(2 * u + 1, pairs, plane_pitch), :]
        upper = jnp.where(low, even, pltpu.roll(odd, cells, 1))
        lower = jnp.where(low, pltpu.roll(even, cells, 1), odd)
        turned.append(cat([upper, lower], 0))
    field = along_rows(column_table[...], cat(turned, 1))
    field = field * cat([inverse[block(u), :] for _, u in every], 1)
    field = along_rows(back_table[...], field)
    for i, (j, u) in enumerate(every):
        upper, lower = field[:pairs, tile(i)], field[pairs:, tile(i)]
        columns[j, pl.ds(2 * u * column_pitch, pairs), :] = jnp.where(low, upper, pltpu.roll(lower, cells, 1))
        columns[j, pl.ds((2 * u + 1) * column_pitch, pairs), :] = jnp.where(low, pltpu.roll(upper, cells, 1), lower)

    parted = CHUNKS if last else 1
    copies = []
    for chunk in range(parted):
        mine = range(chunk * pairs // parted, (chunk + 1) * pairs // parted)
        some = [(j, u) for j in range(sources) for u in mine]
        field = cat([columns[j, pl.ds(u, cells, column_pitch), :] for j, u in some], 1)
        field = along_rows(plane_back_table[order], field)
        field = along_lanes(cat([field[:, tile(i)] for i in range(len(some))], 0))
        result = refs[9] if last else out
        for position, u in enumerate(mine):
            for segment in segments:
                value = 0.0 if first else before[rows(segment), tile(u)]
                for j in range(sources):
                    start = (j * len(mine) + position) * cells + segment * ROWS
                    value = value - piece(j, segment, u) * field[start:start + ROWS]
                result[rows(segment), tile(u)] = value
        if last:
            span = pl.ds(mine[0] * LANES, len(mine) * LANES)
            copy = pltpu.make_async_copy(result.at[:, span], out.at[:, span], refs[10].at[chunk])
            copy.start()
            copies.append(copy)
    for copy in copies:
        copy.wait()


def solve(target, groups, total, constants, last, *earlier):
    cells, plane = target.shape
    vmem = pl.BlockSpec(memory_space=pltpu.VMEM)
    layout = tuple(tuple(part[1:] for part in group) for group in groups)
    operands = [part[0] for group in groups for part in group]
    operands += list(earlier) + [target] + ([] if total is None else [total]) + list(constants)
    operands = [pltpu.with_memory_space_constraint(operand, pltpu.VMEM) for operand in operands]
    shape = (cells, plane)
    scratch = [
        pltpu.VMEM((len(groups), cells // 2 * (cells + 8), LANES), jnp.float32),
        pltpu.VMEM((len(groups), cells * (cells // 2 + 8), LANES), jnp.float32),
    ]
    if last:
        scratch += [pltpu.VMEM(shape, jnp.float32), pltpu.SemaphoreType.DMA((CHUNKS,))]
    return pl.pallas_call(
        functools.partial(solve_kernel, cells, layout, len(earlier), total is None, last),
        out_shape=jax.ShapeDtypeStruct(shape, jnp.float32) if last else pltpu.VMEM(shape, jnp.float32),
        in_specs=[vmem] * len(operands),
        out_specs=pl.BlockSpec(memory_space=pltpu.HBM if last else pltpu.VMEM),
        scratch_shapes=scratch,
        compiler_params=pltpu.CompilerParams(vmem_limit_bytes=32 << 20),
    )(*operands)


def from_member(piece, distance):
    return lax.ppermute(piece, "member", [(i ^ distance, i) for i in range(lax.axis_size("member"))])


def from_band(piece):
    count = lax.axis_size("band")
    return lax.ppermute(piece, "band", [((i - 1) % count, i) for i in range(count)])


def after(value, *earlier):
    return lax.optimization_barrier((value, *earlier))[0]


def body(targets, sources):
    cells = targets.shape[1]
    count, extent = sources.shape[:2]
    members = lax.axis_size("member")
    if members != 4:
        constants = in_vmem([targets[0]] + [jnp.asarray(table) for table in tables(cells, [np.arange(cells)])])
        total = None
        slab = sources
        for stop in range(STOPS):
            if stop > 0:
                slab = from_band(slab)
            whole = lax.all_gather(slab, "member", axis=1, tiled=True)
            for index in range(count):
                last = stop == STOPS - 1 and index == count - 1
                total = solve(constants[0], [[(whole, index, None, 0, cells)]], total, constants[1:], last)
        return total[None]
    member_rows = np.arange(cells).reshape(members, extent)
    layouts = [np.concatenate([member_rows[i ^ k] for k in range(members)]) for i in range(members)]
    everything = [jnp.asarray(table) for table in tables(cells, layouts)]
    mine = in_vmem_parts(sources)
    across, far = [None, None], [None, None]
    across[0] = from_member(mine[0], 2)
    far[1] = from_band(mine[1])
    across[1] = from_member(mine[1], 2)
    near = from_member(sources, 1)
    far[0] = from_band(after(mine[0], near))
    target, *constants = in_vmem([targets[0]] + everything, near)
    across[0], far[1] = after(across[0], target), after(far[1], target)
    far_across = [from_band(across[0]), from_member(far[1], 2)]
    half = extent // 2
    across_near = [[from_member(across[0], 1)], None]
    late = after(across[1], across_near[0][0], far[0])
    across_near[1] = [from_member(late[:, i * half:(i + 1) * half], 1) for i in range(2)]
    groups = [[(mine[i], 0, 0, 0, extent), (near, i, 1, 0, extent), (across[i], 0, 2, 0, extent)] for i in range(2)]
    groups[0] += [(across_near[0][0], 0, 3, 0, extent)]
    groups[1] += [(across_near[1][i], 0, 3, i * half, half) for i in range(2)]
    total = solve(target, groups, None, constants, False, far[0])
    far_near = [from_member(value, 1) for value in far]
    far_across = [after(value, total) for value in far_across]
    far_across_near = [from_member(value, 1) for value in far_across]
    groups = [[(far[i], 0, 0), (far_near[i], 0, 1), (far_across[i], 0, 2), (far_across_near[i], 0, 3)] for i in range(2)]
    groups = [[part + (0, extent) for part in group] for group in groups]
    total = solve(target, groups, total, constants, True)
    return total[None]


def solution(mesh):
    placed = (P(("band", "member"), None, None), P("band", "member", None))
    return jax.shard_map(
        body,
        mesh=mesh,
        in_specs=placed,
        out_specs=P(("band", "member"), None, None),
        check_vma=False,
    )
```

```python
import functools

import jax
import jax.numpy as jnp
import numpy as np
from jax import lax
from jax.experimental import pallas as pl
from jax.experimental.pallas import tpu as pltpu
from jax.sharding import PartitionSpec as P

STOPS = 2
LANES = 128
ROWS = 8
CHUNKS = 2

dot = functools.partial(jnp.dot, preferred_element_type=jnp.float32)


def cat(values, axis):
    return jnp.concatenate(values, axis=axis)


def split(values):
    high = values.astype(jnp.bfloat16)
    low = (values - high.astype(jnp.float32)).astype(jnp.bfloat16)
    return high, low


def tables(cells, layouts):
    wave = np.arange(cells) + 1.0
    sine = np.sin(np.pi * wave[:, None] * wave[None, :] / (cells + 1)).astype(np.float32)
    high = sine.astype(jnp.bfloat16)
    low = (sine - high.astype(np.float32)).astype(jnp.bfloat16)
    none = np.zeros_like(high)
    pair_high = np.block([[high, none], [none, high]])
    pair_low = np.block([[low, none], [none, low]])
    lane_table = np.block([[pair_high, pair_low], [pair_high, pair_low]])
    order = np.concatenate([np.arange(0, cells, 2), np.arange(1, cells, 2)])
    def across_planes(rows):
        return np.concatenate([high[:, rows], high[:, rows], low[:, rows]], 1)

    plane_table = np.stack([np.stack([across_planes(rows) for rows in spans]) for spans in layouts])
    whole = [np.concatenate(spans) for spans in layouts]
    plane_back_table = np.stack([np.concatenate([high[rows], high[rows], low[rows]], 1) for rows in whole])
    column_table = np.concatenate([high[:, order], high[:, order], low[:, order]], 1)
    back_table = np.concatenate([high[order], high[order], low[order]], 1)
    single = 4.0 * np.sin(np.pi * wave / (2.0 * (cells + 1))) ** 2
    eigen = single[:, None, None] + single[None, :, None] + single[None, None, :]
    inverse = (2.0 / (cells + 1)) ** 3 / eigen
    inverse = inverse.reshape(cells // 2, 2, cells, cells).transpose(0, 2, 1, 3)
    inverse = inverse.reshape(cells * cells // 2, 2 * cells).astype(np.float32)
    return lane_table, plane_table, plane_back_table, column_table, back_table, inverse


def prepare_kernel(count, *refs):
    outs, sems = refs[-count - 1:-1], refs[-1]
    copies = [pltpu.make_async_copy(refs[i], outs[i], sems.at[i]) for i in range(count)]
    for copy in copies:
        copy.start()
    for copy in copies:
        copy.wait()


def in_vmem(arrays, *earlier):
    return pl.pallas_call(
        functools.partial(prepare_kernel, len(arrays)),
        out_shape=[pltpu.VMEM(array.shape, array.dtype) for array in arrays],
        in_specs=[pl.BlockSpec(memory_space=pltpu.HBM)] * len(arrays) + [pl.BlockSpec(memory_space=pl.ANY)] * len(earlier),
        out_specs=[pl.BlockSpec(memory_space=pltpu.VMEM)] * len(arrays),
        scratch_shapes=[pltpu.SemaphoreType.DMA((len(arrays),))],
        compiler_params=pltpu.CompilerParams(vmem_limit_bytes=1 << 20),
    )(*[pltpu.with_memory_space_constraint(array, pltpu.HBM) for array in arrays], *earlier)


def parts_kernel(source, *refs):
    outs, sems = refs[:-1], refs[-1]
    copies = [pltpu.make_async_copy(source.at[pl.ds(i, 1)], out, sems.at[i]) for i, out in enumerate(outs)]
    for copy in copies:
        copy.start()
    for copy in copies:
        copy.wait()


def in_vmem_parts(sources):
    count, extent, plane = sources.shape
    return pl.pallas_call(
        parts_kernel,
        out_shape=[pltpu.VMEM((1, extent, plane), sources.dtype)] * count,
        in_specs=[pl.BlockSpec(memory_space=pltpu.HBM)],
        out_specs=[pl.BlockSpec(memory_space=pltpu.VMEM)] * count,
        scratch_shapes=[pltpu.SemaphoreType.DMA((count,))],
        compiler_params=pltpu.CompilerParams(vmem_limit_bytes=1 << 20),
    )(pltpu.with_memory_space_constraint(sources, pltpu.HBM))


def parts_kernel(source, *refs):
    outs, sems = refs[:-1], refs[-1]
    copies = [pltpu.make_async_copy(source.at[pl.ds(i, 1)], out, sems.at[i]) for i, out in enumerate(outs)]
    for copy in copies:
        copy.start()
    for copy in copies:
        copy.wait()


def in_vmem_parts(sources):
    count, extent, plane = sources.shape
    return pl.pallas_call(
        parts_kernel,
        out_shape=[pltpu.VMEM((1, extent, plane), sources.dtype)] * count,
        in_specs=[pl.BlockSpec(memory_space=pltpu.HBM)],
        out_specs=[pl.BlockSpec(memory_space=pltpu.VMEM)] * count,
        scratch_shapes=[pltpu.SemaphoreType.DMA((count,))],
        compiler_params=pltpu.CompilerParams(vmem_limit_bytes=1 << 20),
    )(pltpu.with_memory_space_constraint(sources, pltpu.HBM))


def tile(u):
    return slice(u * LANES, (u + 1) * LANES)


def along_lanes(table, values):
    high, rest = split(values)
    product = dot(cat([high, rest], 1), table[...])
    return product[:, :LANES] + product[:, LANES:]


def along_rows(table, values):
    high, rest = split(values)
    return dot(table, cat([high, rest, high], 0))


def readers(cells, groups, refs):
    pieces = []
    for group in groups:
        pieces.append(refs[:len(group)])
        refs = refs[len(group):]
    me = lax.axis_index("member")
    extent = cells // lax.axis_size("member")
    places = [
        [(number, index, row) for number, (index, _, _, count) in enumerate(group) for row in range(0, count, ROWS)]
        for group in groups
    ]
    layout = [
        (distance, offset + row) for _, distance, offset, count in groups[0] for row in range(0, count, ROWS)
    ]

    def rows(segment):
        distance, offset = layout[segment]
        start = offset if distance is None else (me ^ distance) * extent + offset
        return pl.ds(pl.multiple_of(start, ROWS), ROWS)

    def piece(j, segment, u):
        number, index, row = places[j][segment]
        return pieces[j][number][index, row:row + ROWS, tile(u)]

    return rows, piece, range(len(layout)), 0 if layout[0][0] is None else me, refs


def forward(target, rows, piece, every, segments, lane_table, plane_table):
    field = [target[rows(segment), tile(u)] * piece(j, segment, u) for j, u in every for segment in segments]
    field = along_lanes(lane_table, cat(field, 0))
    count = ROWS * len(segments)
    return along_rows(plane_table, cat([field[i * count:(i + 1) * count] for i in range(len(every))], 1))


def begin_kernel(cells, groups, spare, *refs):
    rows, piece, segments, order, refs = readers(cells, groups, refs)
    target, lane_table, plane_table, planes = refs[spare:]
    every = [(j, u) for j in range(len(groups)) for u in range(cells // 2)]
    field = forward(target, rows, piece, every, segments, lane_table, plane_table[order, 0])
    for i, (j, u) in enumerate(every):
        planes[j, pl.ds(u * cells, cells), :] = field[:, tile(i)]


def begin(target, groups, constants, *earlier):
    cells = target.shape[0]
    layout = tuple(tuple(part[1:] for part in group) for group in groups)
    operands = [part[0] for group in groups for part in group] + list(earlier) + [target] + list(constants[:2])
    operands = [pltpu.with_memory_space_constraint(operand, pltpu.VMEM) for operand in operands]
    vmem = pl.BlockSpec(memory_space=pltpu.VMEM)
    return pl.pallas_call(
        functools.partial(begin_kernel, cells, layout, len(earlier)),
        out_shape=pltpu.VMEM((len(groups), cells // 2 * cells, LANES), jnp.float32),
        in_specs=[vmem] * len(operands),
        out_specs=vmem,
        compiler_params=pltpu.CompilerParams(vmem_limit_bytes=24 << 20),
    )(*operands)


def solve_kernel(cells, groups, begun, first, last, *refs):
    sources = len(groups)
    rows, piece, segments, order, refs = readers(cells, groups, refs)
    if begun:
        ready, refs = refs[0], refs[1:]
    target, refs = refs[0], refs[1:]
    if not first:
        before, refs = refs[0], refs[1:]
    lane_table, plane_table, plane_back_table, column_table, back_table, inverse, out, planes, columns = refs[:9]
    pairs = cells // 2
    plane_pitch, column_pitch = cells + 8, pairs + 8
    low = lax.broadcasted_iota(jnp.int32, (pairs, LANES), 1) < cells
    every = [(j, u) for j in range(sources) for u in range(pairs)]

    def block(u):
        return slice(u * cells, (u + 1) * cells)

    missing = segments[len(segments) // 2:] if begun else segments
    field = forward(target, rows, piece, every, missing, lane_table, plane_table[order, int(begun)])
    for i, (j, u) in enumerate(every):
        part = field[:, tile(i)]
        planes[j, pl.ds(u * plane_pitch, cells), :] = part + ready[j, block(u), :] if begun else part

    turned = []
    for j, u in every:
        even = planes[j, pl.ds(2 * u, pairs, plane_pitch), :]
        odd = planes[j, pl.ds(2 * u + 1, pairs, plane_pitch), :]
        upper = jnp.where(low, even, pltpu.roll(odd, cells, 1))
        lower = jnp.where(low, pltpu.roll(even, cells, 1), odd)
        turned.append(cat([upper, lower], 0))
    field = along_rows(column_table[...], cat(turned, 1))
    field = field * cat([inverse[block(u), :] for _, u in every], 1)
    field = along_rows(back_table[...], field)
    for i, (j, u) in enumerate(every):
        upper, lower = field[:pairs, tile(i)], field[pairs:, tile(i)]
        columns[j, pl.ds(2 * u * column_pitch, pairs), :] = jnp.where(low, upper, pltpu.roll(lower, cells, 1))
        columns[j, pl.ds((2 * u + 1) * column_pitch, pairs), :] = jnp.where(low, pltpu.roll(upper, cells, 1), lower)

    parted = CHUNKS if last else 1
    copies = []
    for chunk in range(parted):
        mine = range(chunk * pairs // parted, (chunk + 1) * pairs // parted)
        some = [(j, u) for j in range(sources) for u in mine]
        field = cat([columns[j, pl.ds(u, cells, column_pitch), :] for j, u in some], 1)
        field = along_rows(plane_back_table[order], field)
        field = along_lanes(lane_table, cat([field[:, tile(i)] for i in range(len(some))], 0))
        result = refs[9] if last else out
        for position, u in enumerate(mine):
            for segment in segments:
                value = 0.0 if first else before[rows(segment), tile(u)]
                for j in range(sources):
                    start = (j * len(mine) + position) * cells + segment * ROWS
                    value = value - piece(j, segment, u) * field[start:start + ROWS]
                result[rows(segment), tile(u)] = value
        if last:
            span = pl.ds(mine[0] * LANES, len(mine) * LANES)
            copy = pltpu.make_async_copy(result.at[:, span], out.at[:, span], refs[10].at[chunk])
            copy.start()
            copies.append(copy)
    for copy in copies:
        copy.wait()


def solve(target, groups, ready, total, constants, last):
    cells, plane = target.shape
    vmem = pl.BlockSpec(memory_space=pltpu.VMEM)
    layout = tuple(tuple(part[1:] for part in group) for group in groups)
    operands = [part[0] for group in groups for part in group]
    operands += ([] if ready is None else [ready]) + [target] + ([] if total is None else [total]) + list(constants)
    operands = [pltpu.with_memory_space_constraint(operand, pltpu.VMEM) for operand in operands]
    shape = (cells, plane)
    scratch = [
        pltpu.VMEM((len(groups), cells // 2 * (cells + 8), LANES), jnp.float32),
        pltpu.VMEM((len(groups), cells * (cells // 2 + 8), LANES), jnp.float32),
    ]
    if last:
        scratch += [pltpu.VMEM(shape, jnp.float32), pltpu.SemaphoreType.DMA((CHUNKS,))]
    return pl.pallas_call(
        functools.partial(solve_kernel, cells, layout, ready is not None, total is None, last),
        out_shape=jax.ShapeDtypeStruct(shape, jnp.float32) if last else pltpu.VMEM(shape, jnp.float32),
        in_specs=[vmem] * len(operands),
        out_specs=pl.BlockSpec(memory_space=pltpu.HBM if last else pltpu.VMEM),
        scratch_shapes=scratch,
        compiler_params=pltpu.CompilerParams(vmem_limit_bytes=32 << 20),
    )(*operands)


def from_member(piece, distance):
    return lax.ppermute(piece, "member", [(i ^ distance, i) for i in range(lax.axis_size("member"))])


def from_band(piece):
    count = lax.axis_size("band")
    return lax.ppermute(piece, "band", [((i - 1) % count, i) for i in range(count)])


def after(value, *earlier):
    return lax.optimization_barrier((value, *earlier))[0]


def body(targets, sources):
    cells = targets.shape[1]
    count, extent = sources.shape[:2]
    members = lax.axis_size("member")
    if members != 4:
        constants = in_vmem([targets[0]] + [jnp.asarray(table) for table in tables(cells, [[np.arange(cells)]])])
        total = None
        slab = sources
        for stop in range(STOPS):
            if stop > 0:
                slab = from_band(slab)
            whole = lax.all_gather(slab, "member", axis=1, tiled=True)
            for index in range(count):
                last = stop == STOPS - 1 and index == count - 1
                total = solve(constants[0], [[(whole, index, None, 0, cells)]], None, total, constants[1:], last)
        return total[None]
    member_rows = np.arange(cells).reshape(members, extent)
    layouts = [
        [np.concatenate([member_rows[i ^ k] for k in span]) for span in ((0, 1), (2, 3))] for i in range(members)
    ]
    everything = [jnp.asarray(table) for table in tables(cells, layouts)]
    mine = in_vmem_parts(sources)
    across, far = [None, None], [None, None]
    across[0] = from_member(mine[0], 2)
    far[1] = from_band(mine[1])
    across[1] = from_member(mine[1], 2)
    near = from_member(sources, 1)
    far[0] = from_band(after(mine[0], near))
    target, *constants = in_vmem([targets[0]] + everything, near)
    ready = begin(target, [[(mine[i], 0, 0, 0, extent), (near, i, 1, 0, extent)] for i in range(2)], constants)
    across[0], far[1] = after(across[0], ready), after(far[1], ready)
    far_across = [from_band(across[0]), from_member(far[1], 2)]
    half = extent // 2
    across_near = [[from_member(across[0], 1)], None]
    soon = across[1]
    late = after(across[1], far[0])
    across_near[1] = [from_member(soon[:, :half], 1), from_member(late[:, half:], 1)]
    groups = [[(mine[i], 0, 0, 0, extent), (near, i, 1, 0, extent), (across[i], 0, 2, 0, extent)] for i in range(2)]
    groups[0] += [(across_near[0][0], 0, 3, 0, extent)]
    groups[1] += [(across_near[1][i], 0, 3, i * half, half) for i in range(2)]
    total = solve(target, groups, ready, None, constants, False)
    far_near = [from_member(value, 1) for value in far]
    ready = begin(target, [[(far[i], 0, 0, 0, extent), (far_near[i], 0, 1, 0, extent)] for i in range(2)], constants, total)
    far_across = [after(value, total) for value in far_across]
    far_across_near = [from_member(value, 1) for value in far_across]
    groups = [[(far[i], 0, 0), (far_near[i], 0, 1), (far_across[i], 0, 2), (far_across_near[i], 0, 3)] for i in range(2)]
    groups = [[part + (0, extent) for part in group] for group in groups]
    total = solve(target, groups, ready, total, constants, True)
    return total[None]


def solution(mesh):
    placed = (P(("band", "member"), None, None), P("band", "member", None))
    return jax.shard_map(
        body,
        mesh=mesh,
        in_specs=placed,
        out_specs=P(("band", "member"), None, None),
        check_vma=False,
    )
```

```python
import functools

import jax
import jax.numpy as jnp
import numpy as np
from jax import lax
from jax.experimental import pallas as pl
from jax.experimental.pallas import tpu as pltpu
from jax.sharding import PartitionSpec as P

STOPS = 2
LANES = 128
ROWS = 8
CHUNKS = 2

dot = functools.partial(jnp.dot, preferred_element_type=jnp.float32)


def cat(values, axis):
    return jnp.concatenate(values, axis=axis)


def split(values):
    high = values.astype(jnp.bfloat16)
    low = (values - high.astype(jnp.float32)).astype(jnp.bfloat16)
    return high, low


def tables(cells, layouts, spans):
    wave = np.arange(cells) + 1.0
    sine = np.sin(np.pi * wave[:, None] * wave[None, :] / (cells + 1)).astype(np.float32)
    high = sine.astype(jnp.bfloat16)
    low = (sine - high.astype(np.float32)).astype(jnp.bfloat16)
    none = np.zeros_like(high)
    pair_high = np.block([[high, none], [none, high]])
    pair_low = np.block([[low, none], [none, low]])
    lane_table = np.block([[pair_high, pair_low], [pair_high, pair_low]])
    order = np.concatenate([np.arange(0, cells, 2), np.arange(1, cells, 2)])
    def across_planes(rows):
        return np.concatenate([high[:, rows], high[:, rows], low[:, rows]], 1)

    plane_tables = [
        np.stack([across_planes(np.concatenate([pieces[k] for k in span])) for pieces in layouts]) for span in spans
    ]
    whole = [np.concatenate(pieces) for pieces in layouts]
    plane_back_table = np.stack([np.concatenate([high[rows], high[rows], low[rows]], 1) for rows in whole])
    column_table = np.concatenate([high[:, order], high[:, order], low[:, order]], 1)
    back_table = np.concatenate([high[order], high[order], low[order]], 1)
    single = 4.0 * np.sin(np.pi * wave / (2.0 * (cells + 1))) ** 2
    eigen = single[:, None, None] + single[None, :, None] + single[None, None, :]
    inverse = (2.0 / (cells + 1)) ** 3 / eigen
    inverse = inverse.reshape(cells // 2, 2, cells, cells).transpose(0, 2, 1, 3)
    inverse = inverse.reshape(cells * cells // 2, 2 * cells).astype(np.float32)
    return lane_table, plane_back_table, column_table, back_table, inverse, *plane_tables


def prepare_kernel(count, *refs):
    outs, sems = refs[-count - 1:-1], refs[-1]
    copies = [pltpu.make_async_copy(refs[i], outs[i], sems.at[i]) for i in range(count)]
    for copy in copies:
        copy.start()
    for copy in copies:
        copy.wait()


def in_vmem(arrays, *earlier):
    return pl.pallas_call(
        functools.partial(prepare_kernel, len(arrays)),
        out_shape=[pltpu.VMEM(array.shape, array.dtype) for array in arrays],
        in_specs=[pl.BlockSpec(memory_space=pltpu.HBM)] * len(arrays) + [pl.BlockSpec(memory_space=pl.ANY)] * len(earlier),
        out_specs=[pl.BlockSpec(memory_space=pltpu.VMEM)] * len(arrays),
        scratch_shapes=[pltpu.SemaphoreType.DMA((len(arrays),))],
        compiler_params=pltpu.CompilerParams(vmem_limit_bytes=1 << 20),
    )(*[pltpu.with_memory_space_constraint(array, pltpu.HBM) for array in arrays], *earlier)


def parts_kernel(source, *refs):
    outs, sems = refs[:-1], refs[-1]
    copies = [pltpu.make_async_copy(source.at[pl.ds(i, 1)], out, sems.at[i]) for i, out in enumerate(outs)]
    for copy in copies:
        copy.start()
    for copy in copies:
        copy.wait()


def in_vmem_parts(sources):
    count, extent, plane = sources.shape
    return pl.pallas_call(
        parts_kernel,
        out_shape=[pltpu.VMEM((1, extent, plane), sources.dtype)] * count,
        in_specs=[pl.BlockSpec(memory_space=pltpu.HBM)],
        out_specs=[pl.BlockSpec(memory_space=pltpu.VMEM)] * count,
        scratch_shapes=[pltpu.SemaphoreType.DMA((count,))],
        compiler_params=pltpu.CompilerParams(vmem_limit_bytes=1 << 20),
    )(pltpu.with_memory_space_constraint(sources, pltpu.HBM))


def parts_kernel(source, *refs):
    outs, sems = refs[:-1], refs[-1]
    copies = [pltpu.make_async_copy(source.at[pl.ds(i, 1)], out, sems.at[i]) for i, out in enumerate(outs)]
    for copy in copies:
        copy.start()
    for copy in copies:
        copy.wait()


def in_vmem_parts(sources):
    count, extent, plane = sources.shape
    return pl.pallas_call(
        parts_kernel,
        out_shape=[pltpu.VMEM((1, extent, plane), sources.dtype)] * count,
        in_specs=[pl.BlockSpec(memory_space=pltpu.HBM)],
        out_specs=[pl.BlockSpec(memory_space=pltpu.VMEM)] * count,
        scratch_shapes=[pltpu.SemaphoreType.DMA((count,))],
        compiler_params=pltpu.CompilerParams(vmem_limit_bytes=1 << 20),
    )(pltpu.with_memory_space_constraint(sources, pltpu.HBM))


def tile(u):
    return slice(u * LANES, (u + 1) * LANES)


def along_lanes(table, values):
    high, rest = split(values)
    product = dot(cat([high, rest], 1), table[...])
    return product[:, :LANES] + product[:, LANES:]


def along_rows(table, values):
    high, rest = split(values)
    return dot(table, cat([high, rest, high], 0))


def readers(cells, groups, refs):
    pieces = []
    for group in groups:
        pieces.append(refs[:len(group)])
        refs = refs[len(group):]
    me = lax.axis_index("member")
    extent = cells // lax.axis_size("member")
    places = [
        [(number, index, row) for number, (index, _, _, count) in enumerate(group) for row in range(0, count, ROWS)]
        for group in groups
    ]
    layout = [
        (distance, offset + row) for _, distance, offset, count in groups[0] for row in range(0, count, ROWS)
    ]

    def rows(segment):
        distance, offset = layout[segment]
        start = offset if distance is None else (me ^ distance) * extent + offset
        return pl.ds(pl.multiple_of(start, ROWS), ROWS)

    def piece(j, segment, u):
        number, index, row = places[j][segment]
        return pieces[j][number][index, row:row + ROWS, tile(u)]

    return rows, piece, range(len(layout)), 0 if layout[0][0] is None else me, refs


def forward(target, rows, piece, every, segments, lane_table, plane_table):
    field = [target[rows(segment), tile(u)] * piece(j, segment, u) for j, u in every for segment in segments]
    field = along_lanes(lane_table, cat(field, 0))
    count = ROWS * len(segments)
    return along_rows(plane_table, cat([field[i * count:(i + 1) * count] for i in range(len(every))], 1))


def begin_kernel(cells, groups, spare, begun, *refs):
    rows, piece, segments, order, refs = readers(cells, groups, refs)
    target, lane_table, plane_table, planes = refs[spare + begun:]
    every = [(j, u) for j in range(len(groups)) for u in range(cells // 2)]
    field = forward(target, rows, piece, every, segments, lane_table, plane_table[order])
    for i, (j, u) in enumerate(every):
        part, here = field[:, tile(i)], pl.ds(u * cells, cells)
        planes[j, here, :] = part + refs[spare][j, here, :] if begun else part


def begin(target, groups, ready, constants, *earlier):
    cells = target.shape[0]
    layout = tuple(tuple(part[1:] for part in group) for group in groups)
    operands = [part[0] for group in groups for part in group] + list(earlier) + ([] if ready is None else [ready])
    operands += [target] + list(constants)
    operands = [pltpu.with_memory_space_constraint(operand, pltpu.VMEM) for operand in operands]
    vmem = pl.BlockSpec(memory_space=pltpu.VMEM)
    return pl.pallas_call(
        functools.partial(begin_kernel, cells, layout, len(earlier), ready is not None),
        out_shape=pltpu.VMEM((len(groups), cells // 2 * cells, LANES), jnp.float32),
        in_specs=[vmem] * len(operands),
        out_specs=vmem,
        compiler_params=pltpu.CompilerParams(vmem_limit_bytes=24 << 20),
    )(*operands)


def solve_kernel(cells, groups, begun, first, last, *refs):
    sources = len(groups)
    rows, piece, segments, order, refs = readers(cells, groups, refs)
    if begun:
        ready, refs = refs[0], refs[1:]
    target, refs = refs[0], refs[1:]
    if not first:
        before, refs = refs[0], refs[1:]
    lane_table, plane_back_table, column_table, back_table, inverse, plane_table, out, planes, columns = refs[:9]
    pairs = cells // 2
    plane_pitch, column_pitch = cells + 8, pairs + 8
    low = lax.broadcasted_iota(jnp.int32, (pairs, LANES), 1) < cells
    every = [(j, u) for j in range(sources) for u in range(pairs)]

    def block(u):
        return slice(u * cells, (u + 1) * cells)

    field = forward(target, rows, piece, every, segments[begun:], lane_table, plane_table[order])
    for i, (j, u) in enumerate(every):
        part = field[:, tile(i)]
        planes[j, pl.ds(u * plane_pitch, cells), :] = part + ready[j, block(u), :] if begun else part

    turned = []
    for j, u in every:
        even = planes[j, pl.ds(2 * u, pairs, plane_pitch), :]
        odd = planes[j, pl.ds(2 * u + 1, pairs, plane_pitch), :]
        upper = jnp.where(low, even, pltpu.roll(odd, cells, 1))
        lower = jnp.where(low, pltpu.roll(even, cells, 1), odd)
        turned.append(cat([upper, lower], 0))
    field = along_rows(column_table[...], cat(turned, 1))
    field = field * cat([inverse[block(u), :] for _, u in every], 1)
    field = along_rows(back_table[...], field)
    for i, (j, u) in enumerate(every):
        upper, lower = field[:pairs, tile(i)], field[pairs:, tile(i)]
        columns[j, pl.ds(2 * u * column_pitch, pairs), :] = jnp.where(low, upper, pltpu.roll(lower, cells, 1))
        columns[j, pl.ds((2 * u + 1) * column_pitch, pairs), :] = jnp.where(low, pltpu.roll(upper, cells, 1), lower)

    parted = CHUNKS if last else 1
    copies = []
    for chunk in range(parted):
        mine = range(chunk * pairs // parted, (chunk + 1) * pairs // parted)
        some = [(j, u) for j in range(sources) for u in mine]
        field = cat([columns[j, pl.ds(u, cells, column_pitch), :] for j, u in some], 1)
        field = along_rows(plane_back_table[order], field)
        field = along_lanes(lane_table, cat([field[:, tile(i)] for i in range(len(some))], 0))
        result = refs[9] if last else out
        for position, u in enumerate(mine):
            for segment in segments:
                value = 0.0 if first else before[rows(segment), tile(u)]
                for j in range(sources):
                    start = (j * len(mine) + position) * cells + segment * ROWS
                    value = value - piece(j, segment, u) * field[start:start + ROWS]
                result[rows(segment), tile(u)] = value
        if last:
            span = pl.ds(mine[0] * LANES, len(mine) * LANES)
            copy = pltpu.make_async_copy(result.at[:, span], out.at[:, span], refs[10].at[chunk])
            copy.start()
            copies.append(copy)
    for copy in copies:
        copy.wait()


def solve(target, groups, ready, total, constants, last):
    cells, plane = target.shape
    vmem = pl.BlockSpec(memory_space=pltpu.VMEM)
    layout = tuple(tuple(part[1:] for part in group) for group in groups)
    planes = constants[-1].shape[-1] // 3
    begun = 0 if ready is None else (cells - planes) // ROWS
    operands = [part[0] for group in groups for part in group]
    operands += ([] if ready is None else [ready]) + [target] + ([] if total is None else [total]) + list(constants)
    operands = [pltpu.with_memory_space_constraint(operand, pltpu.VMEM) for operand in operands]
    shape = (cells, plane)
    scratch = [
        pltpu.VMEM((len(groups), cells // 2 * (cells + 8), LANES), jnp.float32),
        pltpu.VMEM((len(groups), cells * (cells // 2 + 8), LANES), jnp.float32),
    ]
    if last:
        scratch += [pltpu.VMEM(shape, jnp.float32), pltpu.SemaphoreType.DMA((CHUNKS,))]
    return pl.pallas_call(
        functools.partial(solve_kernel, cells, layout, begun, total is None, last),
        out_shape=jax.ShapeDtypeStruct(shape, jnp.float32) if last else pltpu.VMEM(shape, jnp.float32),
        in_specs=[vmem] * len(operands),
        out_specs=pl.BlockSpec(memory_space=pltpu.HBM if last else pltpu.VMEM),
        scratch_shapes=scratch,
        compiler_params=pltpu.CompilerParams(vmem_limit_bytes=32 << 20),
    )(*operands)


def from_member(piece, distance):
    return lax.ppermute(piece, "member", [(i ^ distance, i) for i in range(lax.axis_size("member"))])


def from_band(piece):
    count = lax.axis_size("band")
    return lax.ppermute(piece, "band", [((i - 1) % count, i) for i in range(count)])


def after(value, *earlier):
    return lax.optimization_barrier((value, *earlier))[0]


def body(targets, sources):
    cells = targets.shape[1]
    count, extent = sources.shape[:2]
    members = lax.axis_size("member")
    if members != 4:
        constants = in_vmem([targets[0]] + [jnp.asarray(table) for table in tables(cells, [[np.arange(cells)]], [[0]])])
        total = None
        slab = sources
        for stop in range(STOPS):
            if stop > 0:
                slab = from_band(slab)
            whole = lax.all_gather(slab, "member", axis=1, tiled=True)
            for index in range(count):
                last = stop == STOPS - 1 and index == count - 1
                total = solve(constants[0], [[(whole, index, None, 0, cells)]], None, total, constants[1:], last)
        return total[None]
    member_rows = np.arange(cells).reshape(members, extent)
    layouts = [[member_rows[i ^ k] for k in range(members)] for i in range(members)]
    everything = [jnp.asarray(table) for table in tables(cells, layouts, [(0, 1), (2,), (0, 1, 2), (3,)])]
    mine = in_vmem_parts(sources)
    across, far = [None, None], [None, None]
    across[0] = from_member(mine[0], 2)
    far[1] = from_band(mine[1])
    across[1] = from_member(mine[1], 2)
    near = from_member(sources, 1)
    far[0] = from_band(after(mine[0], near))
    target, lane_table, *constants, own, other, three, rest = in_vmem([targets[0]] + everything, near)
    constants = [lane_table, *constants, rest]
    ready = begin(target, [[(mine[i], 0, 0, 0, extent), (near, i, 1, 0, extent)] for i in range(2)], None, (lane_table, own))
    across[0], far[1] = after(across[0], ready), after(far[1], ready)
    far_across = [from_band(across[0]), from_member(far[1], 2)]
    half = extent // 2
    across_near = [[from_member(across[0], 1)], None]
    soon = across[1]
    ready = begin(target, [[(across[i], 0, 2, 0, extent)] for i in range(2)], ready, (lane_table, other))
    late = after(across[1], far[0], ready)
    across_near[1] = [from_member(soon[:, :half], 1), from_member(late[:, half:], 1)]
    groups = [[(mine[i], 0, 0, 0, extent), (near, i, 1, 0, extent), (across[i], 0, 2, 0, extent)] for i in range(2)]
    groups[0] += [(across_near[0][0], 0, 3, 0, extent)]
    groups[1] += [(across_near[1][i], 0, 3, i * half, half) for i in range(2)]
    total = solve(target, groups, ready, None, constants, False)
    far_near = [from_member(value, 1) for value in far]
    far_across = [after(value, total) for value in far_across]
    far_across_near = [from_member(value, 1) for value in far_across]
    groups = [[(far[i], 0, 0), (far_near[i], 0, 1), (far_across[i], 0, 2), (far_across_near[i], 0, 3)] for i in range(2)]
    groups = [[part + (0, extent) for part in group] for group in groups]
    ready = begin(target, [group[:3] for group in groups], None, (lane_table, three), total)
    total = solve(target, groups, ready, total, constants, True)
    return total[None]


def solution(mesh):
    placed = (P(("band", "member"), None, None), P("band", "member", None))
    return jax.shard_map(
        body,
        mesh=mesh,
        in_specs=placed,
        out_specs=P(("band", "member"), None, None),
        check_vma=False,
    )
```
